256 devices in a mesh: row: 32 (over z, x_hi, core), col: 8 (over x_lo, y).
Axes of the slice: x: 4 (x_hi: 2, x_lo: 2; x = x_hi * 2 + x_lo), y: 4, z: 8, core: 2. Of those that a mesh axis runs over, the one named last changes fastest.
Arguments:
- tokens: bfloat16 [512, 16384], P('row', 'col'), may hold values from -6 to 6
- gate_up: bfloat16 [16384, 2, 28672], P('col', None, 'row'), may hold values from -0.046875 to 0.046875
- down_weight: bfloat16 [28672, 16384], P('row', 'col'), may hold values from -0.03125 to 0.03125
- out_grad: bfloat16 [512, 16384], P('row', 'col'), may hold values from -6 to 6
Outputs:
- block_out: bfloat16 [512, 16384], P('row', 'col')
- grad_tokens: bfloat16 [512, 16384], P('row', 'col')
The draws below stay inside these ranges and needn't reach their ends.
All inputs are finite; a program needn't handle non-finite values.
Results may differ from the reference program's by a relative error of at most 0.0049.
Values may be sent and summed in bfloat16 or wider, within the bound.
No kernel may reach another device: no remote copies, remote signals or barrier semaphores. Data moves between devices by JAX's collectives and lax.ppermute only.
A program may use at most 128 MiB of HBM per device.

```python
import jax
import jax.numpy as jnp
from jax import lax

D = 16384
FF = 28672
TOKENS = 512


def shard_levels(stream_key, dims, split, low, high):
    factor_of = 1.0
    for position, parts in split:
        heights = jax.random.uniform(jax.random.fold_in(jax.random.fold_in(stream_key, 6), position), (parts,), jnp.float32, low / len(split), high / len(split))
        factor_of = factor_of * jnp.repeat(jnp.exp(heights), dims[position] // parts).reshape((-1,) + (1,) * (len(dims) - 1 - position))
    return factor_of


def normal_values(stream_key, shape, scale, reach, cuts=(), kind=jnp.bfloat16):
    values = jax.random.normal(stream_key, shape, jnp.float32) * scale
    if len(cuts) > 0:
        values = shard_levels(stream_key, shape, cuts, -0.22, 0.18) * values
    return jnp.clip(values, min=-reach, max=reach).astype(kind)


def setup_inputs(seed: int = 0) -> dict:
    streams_of = jax.random.split(jax.random.key(seed), 5)
    return {
        "tokens": normal_values(streams_of[0], (TOKENS, D), 1.0, 6.0, ((0, 32), (1, 8))),
        "gate_up": normal_values(streams_of[1], (D, 2, FF), D ** -0.5, 0.046875, ((0, 8), (2, 32))),
        "down_weight": normal_values(streams_of[2], (FF, D), FF ** -0.5, 0.03125, ((0, 32), (1, 8))),
        "out_grad": normal_values(streams_of[3], (TOKENS, D), 1.0, 6.0, ((0, 32), (1, 8))),
    }


def reference(tokens, gate_up, down_weight, out_grad):
    contract_last = (((1,), (1,)), ((), ()))
    gate_vals = jnp.dot(tokens, gate_up[:, 0, :], preferred_element_type=jnp.float32)
    up_vals = jnp.dot(tokens, gate_up[:, 1, :], preferred_element_type=jnp.float32)
    hidden = (jax.nn.silu(gate_vals) * up_vals).astype(jnp.bfloat16)
    block_out = jnp.dot(hidden, down_weight, preferred_element_type=jnp.float32).astype(jnp.bfloat16)
    hid_grad = lax.dot_general(out_grad, down_weight, contract_last, preferred_element_type=jnp.float32)
    squash = jax.nn.sigmoid(gate_vals)
    gate_grad = (hid_grad * up_vals * squash * (1.0 + gate_vals * (1.0 - squash))).astype(jnp.bfloat16)
    up_grad = (hid_grad * gate_vals * squash).astype(jnp.bfloat16)
    first_term = lax.dot_general(gate_grad, gate_up[:, 0, :], contract_last, preferred_element_type=jnp.float32)
    second_term = lax.dot_general(up_grad, gate_up[:, 1, :], contract_last, preferred_element_type=jnp.float32)
    grad_tokens = (first_term + second_term).astype(jnp.bfloat16)
    return block_out, grad_tokens
```

```python
import jax
import jax.numpy as jnp
from jax import lax
from jax.sharding import Mesh, PartitionSpec as P

BF = jnp.bfloat16
F16 = jnp.float16
F32 = jnp.float32
COL = ("xl", "y")
LAST = (((1,), (1,)), ((), ()))
SWAP = [(0, 1), (1, 0)]
NZ = 8
SCALE = 64.0


def shift(x, by):
    return lax.ppermute(x, "z", [(i, (i - by) % NZ) for i in range(NZ)])


def at_z(by):
    return (lax.axis_index("z") + by) & (NZ - 1)


def gather_z(pair, held=None):
    half = pair.shape[0] // 2
    got = {0: pair}
    for r in (1, -1, 2, -2):
        got[r] = shift(pair, r)
    far, held = lax.optimization_barrier(((got[2], got[-2]), held))
    got[3], got[-3] = shift(far[0], 1), shift(far[1], -1)
    got[4] = jnp.concatenate([shift(far[0][:half], 2), shift(far[1][half:], -2)])
    whole = jnp.zeros((NZ,) + pair.shape, pair.dtype)
    for r, block in got.items():
        whole = lax.dynamic_update_slice(whole, block[None], (at_z(r), 0, 0))
    return whole.reshape(-1, pair.shape[1]), held


def swap_core(x):
    return lax.ppermute(x, "core", SWAP)


def scatter_rows(mine, held=None):
    half = mine.shape[0]
    blocks = mine.reshape(NZ, half // NZ, -1)
    rows = half // NZ // 2

    def block(r):
        return lax.dynamic_index_in_dim(blocks, at_z(r), 0, keepdims=False)

    total = block(0)
    seconds = []
    for way in (1, -1):
        far = block(4)[:rows] if way == 1 else block(4)[rows:]
        near = shift(jnp.concatenate([block(way), block(3 * way)]).astype(BF), -way).astype(F32)
        far = shift(far.astype(BF), -2 * way).astype(F32)
        total = total + near[: 2 * rows]
        zero = jnp.zeros_like(far)
        relayed = jnp.concatenate([far, zero] if way == 1 else [zero, far])
        seconds.append((block(2 * way) + near[2 * rows :] + relayed).astype(BF))
    seconds, held = lax.optimization_barrier((seconds, held))
    for way, second in zip((1, -1), seconds):
        total = total + shift(second, -2 * way).astype(F32)
    return (total[:rows] + lax.ppermute(total[rows:].astype(BF), "xh", SWAP).astype(F32)).astype(BF), held


def exchange(x):
    return lax.all_to_all(x, COL, 0, 0, tiled=True)


def copies(x):
    return jnp.broadcast_to(x[None], (8,) + x.shape)


def per_device(tokens, gate_up, down_weight, out_grad):
    width = gate_up.shape[2]
    n = tokens.shape[0]
    weights = gate_up.reshape(gate_up.shape[0], 2 * width)
    other = lax.ppermute(jnp.concatenate([tokens, out_grad]), "xh", SWAP)
    tok, weights = gather_z(jnp.concatenate([tokens, other[:n]]), weights)
    half = tok.shape[0]
    chunk = half // 4

    tok_x = swap_core(tok)
    first = (jnp.dot(tok, weights, preferred_element_type=F32) * SCALE).astype(F16)
    second = (jnp.dot(tok_x, weights, preferred_element_type=F32) * SCALE).astype(F16)
    parts = jnp.concatenate([first, second]).reshape(8, chunk, -1)
    both = exchange(parts)

    pair, _ = lax.optimization_barrier((jnp.concatenate([out_grad, other[n:]]), parts))
    grad, _ = gather_z(pair)
    grad = jnp.concatenate([grad, swap_core(grad)])
    part = lax.dot_general(grad, down_weight, LAST, preferred_element_type=F32)
    part = part.astype(BF).reshape(8, chunk, width)

    both, part = lax.optimization_barrier((both, part))
    both = both.astype(F32).sum(0) * (1.0 / SCALE)
    gate, up = both[:, :width], both[:, width:]
    squash = jax.nn.sigmoid(gate)
    hidden = (gate * squash * up).astype(BF)
    here = exchange(jnp.concatenate([copies(hidden), part], axis=1))
    hidden = here[:, :chunk].reshape(2 * half, width)
    hid_grad = here[:, chunk:].astype(F32).sum(0)

    gate_grad = (hid_grad * up * squash * (1.0 + gate * (1.0 - squash))).astype(BF)
    up_grad = (hid_grad * gate * squash).astype(BF)
    send = copies(jnp.concatenate([gate_grad, up_grad], axis=1))
    send, hidden = lax.optimization_barrier((send, hidden))
    grads = exchange(send).reshape(2 * half, 2 * width)

    out = jnp.dot(hidden, down_weight, preferred_element_type=F32)
    out = out[:half] + swap_core(out[half:].astype(BF)).astype(F32)
    block_out, grads = scatter_rows(out, grads)

    out_x = lax.dot_general(grads[half:], weights, LAST, preferred_element_type=F32).astype(BF)
    mine, out_x = lax.optimization_barrier((grads[:half], out_x))
    out = lax.dot_general(mine, weights, LAST, preferred_element_type=F32)
    grad_tokens, _ = scatter_rows(out + swap_core(out_x).astype(F32))
    return block_out, grad_tokens


def solution(mesh):
    fine = Mesh(mesh.devices.reshape(8, 2, 2, 2, 4), ("z", "xh", "core", "xl", "y"))
    row, col = ("z", "xh", "core"), COL
    return jax.shard_map(
        per_device,
        mesh=fine,
        in_specs=(P(row, col), P(col, None, row), P(row, col), P(row, col)),
        out_specs=(P(row, col), P(row, col)),
        check_vma=False,
    )
```

```python
import jax
import jax.numpy as jnp
from jax import lax
from jax.experimental import pallas as pl
from jax.experimental.pallas import tpu as pltpu
from jax.sharding import Mesh, PartitionSpec as P

BF = jnp.bfloat16
F16 = jnp.float16
F32 = jnp.float32
SWAP = [(0, 1), (1, 0)]
NZ, NY = 8, 4
CUT = 384
SCALE = 64.0
PARAMS = pltpu.CompilerParams(vmem_limit_bytes=58 << 20)


def dot(a, b, turned):
    return lax.dot_general(
        a, b, (((1,), (1 if turned else 0,)), ((), ())), preferred_element_type=F32
    )


def project(tok, grad, weights, down, part, earlier):
    rows, feat = tok.shape
    steps = 7
    wide, narrow = weights.shape[1] // steps, down.shape[0] // steps

    def body(tok_ref, grad_ref, w_ref, d_ref, *refs):
        both_ref, hid_ref = refs[-2:]
        both_ref[...] = dot(tok_ref[...], w_ref[...], False)
        hid_ref[...] = dot(grad_ref[...], d_ref[...], True)

    whole = pl.BlockSpec((rows, feat), lambda i: (0, 0))
    anywhere = pl.BlockSpec(memory_space=pl.ANY)
    return pl.pallas_call(
        body,
        grid=(steps,),
        in_specs=[
            whole,
            whole,
            pl.BlockSpec((feat, wide), lambda i: (0, i)),
            pl.BlockSpec((narrow, feat), lambda i: (i, 0)),
        ]
        + [anywhere] * len(earlier),
        out_specs=[
            pl.BlockSpec((rows, wide), lambda i: (part, i)),
            pl.BlockSpec((rows, narrow), lambda i: (part, i)),
        ],
        out_shape=[
            jax.ShapeDtypeStruct((2 * rows, weights.shape[1]), F32),
            jax.ShapeDtypeStruct((2 * rows, down.shape[0]), F32),
        ],
        input_output_aliases={4: 0, 5: 1} if earlier else {},
        compiler_params=PARAMS,
    )(tok, grad, weights, down, *earlier)


def back(first, second, weights, down, kind):
    rows = first.shape[0]
    feat, units = weights.shape[0], down.shape[0]
    width = 256

    def body(a_ref, b_ref, w_ref, d_ref, out_ref, grad_ref):
        a, b = a_ref[...], b_ref[...]
        n, m = CUT, units - CUT
        w, d = w_ref[...], d_ref[...]
        out_ref[...] = (
            dot(a[:, 2 * n :], d[:n], False) + dot(b[:, 2 * m :], d[n:], False)
        ).astype(kind)
        grad_ref[...] = (
            dot(a[:, :n], w[:, :n], True)
            + dot(a[:, n : 2 * n], w[:, units : units + n], True)
            + dot(b[:, :m], w[:, n:units], True)
            + dot(b[:, m : 2 * m], w[:, units + n :], True)
        ).astype(kind)

    out = pl.BlockSpec((rows, width), lambda i: (0, i))
    return pl.pallas_call(
        body,
        grid=(feat // width,),
        in_specs=[
            pl.BlockSpec(first.shape, lambda i: (0, 0)),
            pl.BlockSpec(second.shape, lambda i: (0, 0)),
            pl.BlockSpec((width, 2 * units), lambda i: (i, 0)),
            pl.BlockSpec((units, width), lambda i: (0, i)),
        ],
        out_specs=[out, out],
        out_shape=[jax.ShapeDtypeStruct((rows, feat), kind)] * 2,
        compiler_params=PARAMS,
    )(first, second, weights, down)


def send(x, axis, by):
    n = lax.axis_size(axis)
    return lax.ppermute(x, axis, [(i, (i + by) % n) for i in range(n)])


def gather_z(pair, held=None):
    half = pair.shape[0] // 2
    got = {0: pair}
    for step in (1, 2, 3):
        got[step] = send(got[step - 1], "z", -1)
        got[-step] = send(got[1 - step], "z", 1)
        if step == 2:
            (got[2], got[-2]), held = lax.optimization_barrier(((got[2], got[-2]), held))
    got[4] = jnp.concatenate([send(got[3][:half], "z", -1), send(got[-3][half:], "z", 1)])
    return jnp.concatenate([got[r] if r <= 4 else got[r - NZ] for r in range(NZ)]), held


def scatter_z(mine):
    blocks = mine.reshape(NZ, mine.shape[0] // NZ, -1)
    half = blocks.shape[1] // 2
    total = blocks[0]
    for way in (1, -1):
        rows = slice(0, half) if way == 1 else slice(half, 2 * half)
        come = send(blocks[4][rows].astype(BF), "z", way).astype(F32)
        zero = jnp.zeros_like(come)
        come = jnp.concatenate([come, zero] if way == 1 else [zero, come])
        for r in (3, 2, 1):
            come = send((blocks[(way * r) % NZ] + come).astype(BF), "z", way).astype(F32)
        total = total + come
    return total


def at_y(x, by, axis):
    return lax.dynamic_index_in_dim(x, (lax.axis_index("y") + by) & (NY - 1), axis, keepdims=False)


def scatter_y(x, axis):
    half = x.shape[-2] // 2
    far = at_y(x, 2, axis).astype(F16)
    up = send(far[..., :half, :], "y", 1).astype(F32)
    down = send(far[..., half:, :], "y", -1).astype(F32)
    zero = jnp.zeros_like(up)
    up = at_y(x, 1, axis).astype(F32) + jnp.concatenate([up, zero], axis=-2)
    down = at_y(x, 3, axis).astype(F32) + jnp.concatenate([zero, down], axis=-2)
    up = send(up.astype(F16), "y", 1).astype(F32)
    return at_y(x, 0, axis).astype(F32) + up + send(down.astype(F16), "y", -1).astype(F32)


def gather_y(x, axis):
    half = x.shape[-2] // 2
    below, above = send(x, "y", 1), send(x, "y", -1)
    far = jnp.concatenate(
        [send(above[..., :half, :], "y", -1), send(below[..., half:, :], "y", 1)], axis=-2
    )
    whole = jnp.zeros(x.shape[:axis] + (NY,) + x.shape[axis:], x.dtype)
    for by, block in ((0, x), (-1, below), (1, above), (2, far)):
        at = [0] * whole.ndim
        at[axis] = (lax.axis_index("y") + by) & (NY - 1)
        whole = lax.dynamic_update_slice(whole, jnp.expand_dims(block, axis), at)
    return whole


def gate(total):
    gate_vals, up_vals, hid_grad = jnp.split(total * (1.0 / SCALE), 3, axis=1)
    squash = jax.nn.sigmoid(gate_vals)
    gate_grad = hid_grad * up_vals * squash * (1.0 + gate_vals * (1.0 - squash))
    parts = (gate_grad, hid_grad * gate_vals * squash, gate_vals * squash * up_vals)
    return jnp.concatenate([part.astype(BF) for part in parts], axis=1)


def per_device(tokens, gate_up, down_weight, out_grad):
    units = gate_up.shape[2]
    n = tokens.shape[0]
    low = lax.axis_index("xl") == 0
    weights = gate_up.reshape(gate_up.shape[0], 2 * units)

    other = lax.ppermute(jnp.concatenate([tokens, out_grad]), "xh", SWAP)
    other, weights = lax.optimization_barrier((other, weights))
    tok, weights = gather_z(jnp.concatenate([tokens, other[:n]]), weights)
    grad, _ = gather_z(jnp.concatenate([out_grad, other[n:]]))
    half = tok.shape[0]

    earlier = project(tok, grad, weights, down_weight, 0, ())
    tok, grad = send(tok, "core", 1), send(grad, "core", 1)
    both, hid = project(tok, grad, weights, down_weight, 1, earlier)

    def columns(lo, hi):
        cols = [both[:, lo:hi], both[:, units + lo : units + hi], hid[:, lo:hi]]
        return (jnp.concatenate(cols, axis=1) * SCALE).astype(F16).reshape(2, NY, half // NY, -1)

    a, b = columns(0, CUT), columns(CUT, units)
    keep, give = jnp.where(low, a[0], a[1]), jnp.where(low, a[1], a[0])
    a = scatter_y(keep.astype(F32) + send(give, "xl", 1).astype(F32), 0)
    b = scatter_y(b, 1)
    keep, give = jnp.where(low, b[0], b[1]), jnp.where(low, b[1], b[0])
    b = keep + send(give.astype(F16), "xl", 1).astype(F32)

    a, b = gate(a), gate(b)
    a = gather_y(a, 0).reshape(half, -1)
    come = send(a, "xl", 1)
    a = jnp.where(low, a, come), jnp.where(low, come, a)
    come = send(b, "xl", 1)
    b = gather_y(jnp.where(low, jnp.stack([b, come]), jnp.stack([come, b])), 1)
    b = b.reshape(2, half, -1)

    sent = back(a[1], b[1], weights, down_weight, BF)
    mine, sent = lax.optimization_barrier(((a[0], b[0]), sent))
    kept = back(*mine, weights, down_weight, F32)
    sums = [scatter_z(k + send(s, "core", 1).astype(F32)) for k, s in zip(kept, sent)]
    come = lax.ppermute(jnp.concatenate([s[n:] for s in sums]).astype(BF), "xh", SWAP).astype(F32)
    return (sums[0][:n] + come[:n]).astype(BF), (sums[1][:n] + come[n:]).astype(BF)


def solution(mesh):
    fine = Mesh(mesh.devices.reshape(8, 2, 2, 2, 4), ("z", "xh", "core", "xl", "y"))
    row, col = ("z", "xh", "core"), ("xl", "y")
    return jax.shard_map(
        per_device,
        mesh=fine,
        in_specs=(P(row, col), P(col, None, row), P(row, col), P(row, col)),
        out_specs=(P(row, col), P(row, col)),
        check_vma=False,
    )
```

```python
import jax
import jax.numpy as jnp
from jax import lax
from jax.sharding import Mesh, PartitionSpec as P

BF = jnp.bfloat16
F16 = jnp.float16
F32 = jnp.float32
COL = ("xl", "y")
LAST = (((1,), (1,)), ((), ()))
SWAP = [(0, 1), (1, 0)]
NZ = 8
SCALE = 64.0


def shift(x, by):
    return lax.ppermute(x, "z", [(i, (i - by) % NZ) for i in range(NZ)])


def at_z(by):
    return (lax.axis_index("z") + by) & (NZ - 1)


def gather_z(pair):
    half = pair.shape[0] // 2
    got = {0: pair}
    for r in (1, -1, 2, -2):
        got[r] = shift(pair, r)
    got[3], got[-3] = shift(got[2], 1), shift(got[-2], -1)
    got[4] = jnp.concatenate([shift(got[2][:half], 2), shift(got[-2][half:], -2)])
    whole = jnp.zeros((NZ,) + pair.shape, pair.dtype)
    for r, block in got.items():
        whole = lax.dynamic_update_slice(whole, block[None], (at_z(r), 0, 0))
    return whole.reshape(-1, pair.shape[1])


def swap_core(x):
    return lax.ppermute(x, "core", SWAP)


def scatter_rows(mine, held=None):
    half = mine.shape[0]
    blocks = mine.reshape(NZ, half // NZ, -1)
    rows = half // NZ // 2

    def block(r):
        return lax.dynamic_index_in_dim(blocks, at_z(r), 0, keepdims=False)

    total = block(0)
    seconds = []
    for way in (1, -1):
        far = block(4)[:rows] if way == 1 else block(4)[rows:]
        near = shift(jnp.concatenate([block(way), block(3 * way)]).astype(BF), -way).astype(F32)
        far = shift(far.astype(BF), -2 * way).astype(F32)
        total = total + near[: 2 * rows]
        zero = jnp.zeros_like(far)
        relayed = jnp.concatenate([far, zero] if way == 1 else [zero, far])
        seconds.append((block(2 * way) + near[2 * rows :] + relayed).astype(BF))
    seconds = [shift(second, -2 * way) for way, second in zip((1, -1), seconds)]
    seconds, held = lax.optimization_barrier((seconds, held))
    total = total + seconds[0].astype(F32) + seconds[1].astype(F32)
    return (total[:rows] + lax.ppermute(total[rows:].astype(BF), "xh", SWAP).astype(F32)).astype(BF), held


def exchange(x):
    return lax.all_to_all(x, COL, 0, 0, tiled=True)


def copies(x):
    return jnp.broadcast_to(x[None], (8,) + x.shape)


def col_pairs():
    xl, y = lax.axis_index("xl"), lax.axis_index("y")
    for dx, dy in ((1, 0), (0, 1), (0, 3), (1, 1), (1, 3), (0, 2), (1, 2)):
        perm = [(4 * i + j, 4 * ((i + dx) % 2) + (j + dy) % 4) for i in range(2) for j in range(4)]
        yield 4 * (xl ^ dx) + ((y - dy) & 3), perm


def per_device(tokens, gate_up, down_weight, out_grad):
    width = gate_up.shape[2]
    n = tokens.shape[0]
    weights = gate_up.reshape(gate_up.shape[0], 2 * width)
    other = lax.ppermute(jnp.concatenate([tokens, out_grad]), "xh", SWAP)
    tok = gather_z(jnp.concatenate([tokens, other[:n]]))
    half = tok.shape[0]
    chunk = half // 4

    tok = jnp.concatenate([tok, swap_core(tok)])
    parts = (jnp.dot(tok, weights, preferred_element_type=F32) * SCALE).astype(F16)
    both = exchange(parts.reshape(8, chunk, -1))

    pair, _ = lax.optimization_barrier((jnp.concatenate([out_grad, other[n:]]), parts))
    grad = gather_z(pair)
    grad = jnp.concatenate([grad, swap_core(grad)])
    part = lax.dot_general(grad, down_weight, LAST, preferred_element_type=F32)
    part = (part * SCALE).astype(F16).reshape(8, chunk, width)

    both, part = lax.optimization_barrier((both, part))
    hid_grad = exchange(part)
    both = both.astype(F32).sum(0) * (1.0 / SCALE)
    gate, up = both[:, :width], both[:, width:]
    squash = jax.nn.sigmoid(gate)
    hidden = (gate * squash * up).astype(BF)
    got = [lax.ppermute(hidden, COL, perm) for _, perm in col_pairs()]
    hid_grad, got = lax.optimization_barrier((hid_grad, got))
    hid_grad = hid_grad.astype(F32).sum(0) * (1.0 / SCALE)

    gate_grad = (hid_grad * up * squash * (1.0 + gate * (1.0 - squash))).astype(BF)
    up_grad = (hid_grad * gate * squash).astype(BF)
    send = copies(jnp.concatenate([gate_grad, up_grad], axis=1))
    send, got = lax.optimization_barrier((send, got))
    grads = exchange(send).reshape(2 * half, 2 * width)
    me = 4 * lax.axis_index("xl") + lax.axis_index("y")
    whole = lax.dynamic_update_slice(jnp.zeros((8, chunk, width), BF), hidden[None], (me, 0, 0))
    for x, (came, _) in zip(got, col_pairs()):
        whole = lax.dynamic_update_slice(whole, x[None], (came, 0, 0))
    hidden = whole.reshape(2 * half, width)

    out = jnp.dot(hidden, down_weight, preferred_element_type=F32)
    out = out[:half] + swap_core(out[half:].astype(BF)).astype(F32)
    block_out, grads = scatter_rows(out, grads)

    out_x = lax.dot_general(grads[half:], weights, LAST, preferred_element_type=F32).astype(BF)
    mine, out_x = lax.optimization_barrier((grads[:half], out_x))
    out = lax.dot_general(mine, weights, LAST, preferred_element_type=F32)
    grad_tokens, _ = scatter_rows(out + swap_core(out_x).astype(F32))
    return block_out, grad_tokens


def solution(mesh):
    fine = Mesh(mesh.devices.reshape(8, 2, 2, 2, 4), ("z", "xh", "core", "xl", "y"))
    row, col = ("z", "xh", "core"), COL
    return jax.shard_map(
        per_device,
        mesh=fine,
        in_specs=(P(row, col), P(col, None, row), P(row, col), P(row, col)),
        out_specs=(P(row, col), P(row, col)),
        check_vma=False,
    )
```

```python
import jax
import jax.numpy as jnp
from jax import lax
from jax.sharding import Mesh, PartitionSpec as P

BF = jnp.bfloat16
F16 = jnp.float16
F32 = jnp.float32
ROW, COL = ("z", "xh", "core"), ("xl", "y")
LAST = (((1,), (1,)), ((), ()))
SWAP = [(0, 1), (1, 0)]
NZ = 8
SCALE = 64.0


def swap(x, axis):
    return lax.ppermute(x, axis, SWAP)


def onward(x):
    perm = [(2 * i + c, 2 * ((i + 1 - 2 * c) % NZ) + c) for i in range(NZ) for c in range(2)]
    return lax.ppermute(x, ("z", "core"), perm)


def gather_z(block, after=None):
    got = [block, onward(block)]
    got[1], _ = lax.optimization_barrier((got[1], after))
    for _ in range(2):
        got.append(onward(got[-1]))
    got.append(onward(got[3][: block.shape[0] // 2]))
    behind = jnp.concatenate(got[1:])
    return jnp.concatenate([block, behind, swap(behind, "core")])


def scatter_rows(p, held=None):
    n = p.shape[0] // 8
    end = n + (p.shape[0] - n) // 2
    ahead = p[end:] + swap(p[n:end].astype(BF), "core").astype(F32)
    come = onward(ahead[3 * n :].astype(BF)).astype(F32)
    come = jnp.concatenate([come, jnp.zeros_like(come)])
    for k in (2, 1, 0):
        come = onward((ahead[k * n : (k + 1) * n] + come).astype(BF))
        if k > 0:
            come = come.astype(F32)
    come, held = lax.optimization_barrier((come, held))
    come = come.astype(F32)
    m = n // 2
    give = (p[m:n] + come[:m]).astype(BF)
    mine = p[:m] + come[m:] + swap(give, "core").astype(F32)
    m = m // 2
    return (mine[:m] + swap(mine[m:].astype(BF), "xh").astype(F32)).astype(BF), held


def exchange(x):
    return lax.all_to_all(x, COL, 0, 0, tiled=True)


def copies(x):
    return jnp.broadcast_to(x[None], (8,) + x.shape)


def per_device(tokens, gate_up, down_weight, out_grad):
    width = gate_up.shape[2]
    n = tokens.shape[0]
    weights = gate_up.reshape(gate_up.shape[0], 2 * width)

    other = swap(jnp.concatenate([tokens, out_grad]), "xh")
    mine = jnp.concatenate([tokens, other[:n], out_grad, other[n:]])
    other = swap(mine, "core")
    tok = gather_z(jnp.concatenate([mine[: 2 * n], other[: 2 * n]]))
    rows = tok.shape[0]
    chunk = rows // 8
    parts = (jnp.dot(tok, weights, preferred_element_type=F32) * SCALE).astype(F16)
    parts = parts.reshape(8, chunk, -1)
    both = exchange(parts)

    block = jnp.concatenate([mine[2 * n :], other[2 * n :]])
    block, _ = lax.optimization_barrier((block, tok))
    grad = gather_z(block, parts)
    part = lax.dot_general(grad, down_weight, LAST, preferred_element_type=F32)
    part = part.astype(BF).reshape(8, chunk, width)

    both, part = lax.optimization_barrier((both, part))
    both = both.astype(F32).sum(0) * (1.0 / SCALE)
    gate, up = both[:, :width], both[:, width:]
    squash = jax.nn.sigmoid(gate)
    hidden = (gate * squash * up).astype(BF)
    here = exchange(jnp.concatenate([copies(hidden), part], axis=1))
    hidden = here[:, :chunk].reshape(rows, width)
    hid_grad = here[:, chunk:].astype(F32).sum(0)

    gate_grad = (hid_grad * up * squash * (1.0 + gate * (1.0 - squash))).astype(BF)
    up_grad = (hid_grad * gate * squash).astype(BF)
    send = copies(jnp.concatenate([gate_grad, up_grad], axis=1))
    send, hidden = lax.optimization_barrier((send, hidden))
    grads = exchange(send).reshape(rows, 2 * width)

    out = jnp.dot(hidden, down_weight, preferred_element_type=F32)
    block_out, grads = scatter_rows(out, grads)
    out = lax.dot_general(grads, weights, LAST, preferred_element_type=F32)
    grad_tokens, _ = scatter_rows(out)
    return block_out, grad_tokens


def solution(mesh):
    fine = Mesh(mesh.devices.reshape(8, 2, 2, 2, 4), ("z", "xh", "core", "xl", "y"))
    return jax.shard_map(
        per_device,
        mesh=fine,
        in_specs=(P(ROW, COL), P(COL, None, ROW), P(ROW, COL), P(ROW, COL)),
        out_specs=(P(ROW, COL), P(ROW, COL)),
        check_vma=False,
    )
```

```python
import jax
import jax.numpy as jnp
from jax import lax
from jax.experimental import pallas as pl
from jax.experimental.pallas import tpu as pltpu
from jax.sharding import Mesh, PartitionSpec as P

BF = jnp.bfloat16
F16 = jnp.float16
F32 = jnp.float32
ROW, COL = ("z", "xh", "core"), ("xl", "y")
LAST = (((1,), (1,)), ((), ()))
SWAP = [(0, 1), (1, 0)]
NZ = 8
SCALE = 64.0


def product(xs, w, turned, types, width):
    depth = xs[0].shape[1]
    n = w.shape[0] if turned else w.shape[1]
    dims = (((1,), (1 if turned else 0,)), ((), ()))

    def body(*refs):
        w_ref = refs[len(xs)]
        for x_ref, o_ref in zip(refs, refs[len(xs) + 1 :]):
            o_ref[...] = lax.dot_general(
                x_ref[...], w_ref[...], dims, preferred_element_type=F32
            ).astype(o_ref.dtype)

    if turned:
        w_spec = pl.BlockSpec((width, depth), lambda i: (i, 0))
    else:
        w_spec = pl.BlockSpec((depth, width), lambda i: (0, i))
    rows = sum(x.shape[0] for x in xs)
    return pl.pallas_call(
        body,
        grid=(n // width,),
        in_specs=[pl.BlockSpec(x.shape, lambda i: (0, 0)) for x in xs] + [w_spec],
        out_specs=[pl.BlockSpec((x.shape[0], width), lambda i: (0, i)) for x in xs],
        out_shape=[jax.ShapeDtypeStruct((x.shape[0], n), t) for x, t in zip(xs, types)],
        compiler_params=pltpu.CompilerParams(vmem_limit_bytes=40 << 20),
        cost_estimate=pl.CostEstimate(
            flops=2 * rows * depth * n,
            bytes_accessed=2 * (w.size + rows * depth + rows * n),
            transcendentals=0,
        ),
    )(*xs, w)


def swap(x, axis):
    return lax.ppermute(x, axis, SWAP)


def shift(x, by):
    return lax.ppermute(x, "z", [(i, (i - by) % NZ) for i in range(NZ)])


def gather_z(pair):
    half = pair.shape[0] // 2
    got = {0: pair}
    for step in (1, 2, 3):
        got[step] = shift(got[step - 1], 1)
        got[-step] = shift(got[1 - step], -1)
    got[4] = jnp.concatenate([shift(got[3][:half], 1), shift(got[-3][half:], -1)])
    return jnp.concatenate([got[r] if r <= 4 else got[r - NZ] for r in range(NZ)])


def scatter_rows(mine, held=None):
    block = mine.reshape(NZ, mine.shape[0] // NZ, -1)
    rows = block.shape[1] // 2
    total = block[0]
    seconds = []
    for way in (1, -1):
        far = block[4][:rows] if way == 1 else block[4][rows:]
        near = jnp.concatenate([block[way % NZ], block[3 * way % NZ]]).astype(BF)
        near = shift(near, -way).astype(F32)
        far = shift(far.astype(BF), -2 * way).astype(F32)
        total = total + near[: 2 * rows]
        zero = jnp.zeros_like(far)
        relayed = jnp.concatenate([far, zero] if way == 1 else [zero, far])
        second = block[2 * way % NZ] + near[2 * rows :] + relayed
        seconds.append(shift(second.astype(BF), -2 * way))
    seconds, held = lax.optimization_barrier((seconds, held))
    total = total + seconds[0].astype(F32) + seconds[1].astype(F32)
    return (total[:rows] + swap(total[rows:].astype(BF), "xh").astype(F32)).astype(BF), held


def exchange(x):
    return lax.all_to_all(x, COL, 0, 0, tiled=True)


def copies(x):
    return jnp.broadcast_to(x[None], (8,) + x.shape)


def per_device(tokens, gate_up, down_weight, out_grad):
    width = gate_up.shape[2]
    n = tokens.shape[0]
    weights = gate_up.reshape(gate_up.shape[0], 2 * width)

    other = swap(jnp.concatenate([tokens, out_grad]), "xh")
    tok = gather_z(jnp.concatenate([tokens, other[:n]]))
    grad = gather_z(jnp.concatenate([out_grad, other[n:]]))
    half = tok.shape[0]
    chunk = half // 4

    tok = jnp.concatenate([tok, swap(tok, "core")])
    parts = (jnp.dot(tok, weights, preferred_element_type=F32) * SCALE).astype(F16)
    both = exchange(parts.reshape(8, chunk, -1))
    part = jnp.concatenate(
        product([grad, swap(grad, "core")], down_weight, True, (BF, BF), 128)
    ).reshape(8, chunk, width)

    both = both.astype(F32).sum(0) * (1.0 / SCALE)
    gate, up = both[:, :width], both[:, width:]
    squash = jax.nn.sigmoid(gate)
    hidden = (gate * squash * up).astype(BF)
    here = exchange(jnp.concatenate([copies(hidden), part], axis=1))
    hid_grad = here[:, chunk:].astype(F32).sum(0)

    gate_grad = (hid_grad * up * squash * (1.0 + gate * (1.0 - squash))).astype(BF)
    up_grad = (hid_grad * gate * squash).astype(BF)
    send = copies(jnp.concatenate([gate_grad, up_grad], axis=1))
    hidden = [here[i : i + 4, :chunk].reshape(half, width) for i in (0, 4)]
    send, hidden = lax.optimization_barrier((send, hidden))
    grads = exchange(send).reshape(2 * half, 2 * width)

    kept, sent = product(hidden, down_weight, False, (F32, BF), 512)
    block_out, grads = scatter_rows(kept + swap(sent, "core").astype(F32), grads)
    out, sent = product([grads[:half], grads[half:]], weights, True, (F32, BF), 256)
    out = out + swap(sent, "core").astype(F32)
    grad_tokens, _ = scatter_rows(out)
    return block_out, grad_tokens


def solution(mesh):
    fine = Mesh(mesh.devices.reshape(8, 2, 2, 2, 4), ("z", "xh", "core", "xl", "y"))
    return jax.shard_map(
        per_device,
        mesh=fine,
        in_specs=(P(ROW, COL), P(COL, None, ROW), P(ROW, COL), P(ROW, COL)),
        out_specs=(P(ROW, COL), P(ROW, COL)),
        check_vma=False,
    )
```

```python
import jax
import jax.numpy as jnp
from jax import lax
from jax.experimental import pallas as pl
from jax.experimental.pallas import tpu as pltpu
from jax.sharding import Mesh, PartitionSpec as P

BF = jnp.bfloat16
F16 = jnp.float16
F32 = jnp.float32
ROW, COL = ("z", "xh", "core"), ("xl", "y")
LAST = (((1,), (1,)), ((), ()))
SWAP = [(0, 1), (1, 0)]
NZ = 8
SCALE = 64.0


def product(xs, w, turned, types, width):
    depth = xs[0].shape[1]
    n = w.shape[0] if turned else w.shape[1]
    dims = (((1,), (1 if turned else 0,)), ((), ()))

    def body(*refs):
        w_ref = refs[len(xs)]
        for x_ref, o_ref in zip(refs, refs[len(xs) + 1 :]):
            o_ref[...] = lax.dot_general(
                x_ref[...], w_ref[...], dims, preferred_element_type=F32
            ).astype(o_ref.dtype)

    if turned:
        w_spec = pl.BlockSpec((width, depth), lambda i: (i, 0))
    else:
        w_spec = pl.BlockSpec((depth, width), lambda i: (0, i))
    rows = sum(x.shape[0] for x in xs)
    return pl.pallas_call(
        body,
        grid=(n // width,),
        in_specs=[pl.BlockSpec(x.shape, lambda i: (0, 0)) for x in xs] + [w_spec],
        out_specs=[pl.BlockSpec((x.shape[0], width), lambda i: (0, i)) for x in xs],
        out_shape=[jax.ShapeDtypeStruct((x.shape[0], n), t) for x, t in zip(xs, types)],
        compiler_params=pltpu.CompilerParams(vmem_limit_bytes=40 << 20),
        cost_estimate=pl.CostEstimate(
            flops=2 * rows * depth * n,
            bytes_accessed=2 * (w.size + rows * depth + rows * n),
            transcendentals=0,
        ),
    )(*xs, w)


def swap(x, axis):
    return lax.ppermute(x, axis, SWAP)


def shift(x, by):
    return lax.ppermute(x, "z", [(i, (i - by) % NZ) for i in range(NZ)])


def gather_z(block):
    half = block.shape[0] // 2
    got = {0: block}
    for step in (1, 2, 3):
        got[step] = shift(got[step - 1], 1)
        got[-step] = shift(got[1 - step], -1)
    first = [got[r][:half] for r in range(4)] + [shift(got[3][:half], 1)]
    second = [got[r][half:] for r in range(4)] + [shift(got[-3][half:], -1)]
    first += [got[r][:half] for r in (-3, -2, -1)]
    second += [got[r][half:] for r in (-3, -2, -1)]
    return jnp.concatenate(first), jnp.concatenate(second)


def scatter_rows(mine, held=None):
    block = mine.reshape(NZ, mine.shape[0] // NZ, -1)
    rows = block.shape[1] // 2
    total = block[0]
    seconds = []
    for way in (1, -1):
        far = block[4][:rows] if way == 1 else block[4][rows:]
        near = jnp.concatenate([block[way % NZ], block[3 * way % NZ]]).astype(BF)
        near = shift(near, -way).astype(F32)
        far = shift(far.astype(BF), -2 * way).astype(F32)
        total = total + near[: 2 * rows]
        zero = jnp.zeros_like(far)
        relayed = jnp.concatenate([far, zero] if way == 1 else [zero, far])
        seconds.append((block[2 * way % NZ] + near[2 * rows :] + relayed).astype(BF))
    seconds, held = lax.optimization_barrier((seconds, held))
    for way, second in zip((1, -1), seconds):
        total = total + shift(second, -2 * way).astype(F32)
    return (total[:rows] + swap(total[rows:].astype(BF), "xh").astype(F32)).astype(BF), held


def exchange(x):
    return lax.all_to_all(x, COL, 0, 0, tiled=True)


def copies(x):
    return jnp.broadcast_to(x[None], (8,) + x.shape)


def per_device(tokens, gate_up, down_weight, out_grad):
    width = gate_up.shape[2]
    n = tokens.shape[0]
    weights = gate_up.reshape(gate_up.shape[0], 2 * width)

    other = swap(jnp.concatenate([tokens, out_grad]), "xh")
    tok, grad = gather_z(jnp.concatenate([tokens, other[:n], out_grad, other[n:]]))
    half = tok.shape[0]
    chunk = half // 4

    tok = jnp.concatenate([tok, swap(tok, "core")])
    parts = (jnp.dot(tok, weights, preferred_element_type=F32) * SCALE).astype(F16)
    both = exchange(parts.reshape(8, chunk, -1))
    part = jnp.concatenate(
        product([grad, swap(grad, "core")], down_weight, True, (BF, BF), width)
    ).reshape(8, chunk, width)

    both = both.astype(F32).sum(0) * (1.0 / SCALE)
    gate, up = both[:, :width], both[:, width:]
    squash = jax.nn.sigmoid(gate)
    hidden = (gate * squash * up).astype(BF)
    here = exchange(jnp.concatenate([copies(hidden), part], axis=1))
    hid_grad = here[:, chunk:].astype(F32).sum(0)

    gate_grad = (hid_grad * up * squash * (1.0 + gate * (1.0 - squash))).astype(BF)
    up_grad = (hid_grad * gate * squash).astype(BF)
    send = copies(jnp.concatenate([gate_grad, up_grad], axis=1))
    hidden = [here[i : i + 4, :chunk].reshape(half, width) for i in (0, 4)]
    send, hidden = lax.optimization_barrier((send, hidden))
    grads = exchange(send).reshape(2 * half, 2 * width)

    kept, sent = product(hidden, down_weight, False, (F32, BF), 512)
    block_out, grads = scatter_rows(kept + swap(sent, "core").astype(F32), grads)
    out = lax.dot_general(grads, weights, LAST, preferred_element_type=F32)
    out = out[:half] + swap(out[half:].astype(BF), "core").astype(F32)
    grad_tokens, _ = scatter_rows(out)
    return block_out, grad_tokens


def solution(mesh):
    fine = Mesh(mesh.devices.reshape(8, 2, 2, 2, 4), ("z", "xh", "core", "xl", "y"))
    return jax.shard_map(
        per_device,
        mesh=fine,
        in_specs=(P(ROW, COL), P(COL, None, ROW), P(ROW, COL), P(ROW, COL)),
        out_specs=(P(ROW, COL), P(ROW, COL)),
        check_vma=False,
    )
```

```python
import jax
import jax.numpy as jnp
from jax import lax
from jax.experimental import pallas as pl
from jax.experimental.pallas import tpu as pltpu
from jax.sharding import Mesh, PartitionSpec as P

BF = jnp.bfloat16
F16 = jnp.float16
F32 = jnp.float32
ROW, COL = ("z", "xh", "core"), ("xl", "y")
LAST = (((1,), (1,)), ((), ()))
SWAP = [(0, 1), (1, 0)]
NZ = 8
SCALE = 64.0


def product(xs, w, turned, types, width):
    depth = xs[0].shape[1]
    n = w.shape[0] if turned else w.shape[1]
    dims = (((1,), (1 if turned else 0,)), ((), ()))

    def body(*refs):
        w_ref = refs[len(xs)]
        for x_ref, o_ref in zip(refs, refs[len(xs) + 1 :]):
            o_ref[...] = lax.dot_general(
                x_ref[...], w_ref[...], dims, preferred_element_type=F32
            ).astype(o_ref.dtype)

    if turned:
        w_spec = pl.BlockSpec((width, depth), lambda i: (i, 0))
    else:
        w_spec = pl.BlockSpec((depth, width), lambda i: (0, i))
    rows = sum(x.shape[0] for x in xs)
    return pl.pallas_call(
        body,
        grid=(n // width,),
        in_specs=[pl.BlockSpec(x.shape, lambda i: (0, 0)) for x in xs] + [w_spec],
        out_specs=[pl.BlockSpec((x.shape[0], width), lambda i: (0, i)) for x in xs],
        out_shape=[jax.ShapeDtypeStruct((x.shape[0], n), t) for x, t in zip(xs, types)],
        compiler_params=pltpu.CompilerParams(vmem_limit_bytes=40 << 20),
        cost_estimate=pl.CostEstimate(
            flops=rows, bytes_accessed=rows * depth,
            transcendentals=0,
        ),
    )(*xs, w)


def swap(x, axis):
    return lax.ppermute(x, axis, SWAP)


def shift(x, by):
    return lax.ppermute(x, "z", [(i, (i - by) % NZ) for i in range(NZ)])


def together(first, second, ready):
    n = first.shape[0]

    def body(a_ref, b_ref, _, out_ref):
        out_ref[:n] = a_ref[...]
        out_ref[n:] = b_ref[...]

    block = pl.BlockSpec(first.shape, lambda: (0, 0))
    return pl.pallas_call(
        body,
        in_specs=[block, block, pl.BlockSpec(memory_space=pl.ANY)],
        out_specs=pl.BlockSpec((2 * n, first.shape[1]), lambda: (0, 0)),
        out_shape=jax.ShapeDtypeStruct((2 * n, first.shape[1]), first.dtype),
        cost_estimate=pl.CostEstimate(flops=1, bytes_accessed=6 * first.size, transcendentals=0),
    )(first, second, ready)


def gather_z(pair, even):
    half = pair.shape[0] // 2
    got = {0: pair}
    for r in (2, -2, 1, -1):
        got[r] = shift(pair, r)
    got[3], got[-3] = shift(got[2], 1), shift(got[-2], -1)
    if even:
        got[4] = jnp.concatenate([shift(got[2][:half], 2), shift(got[-2][half:], -2)])
    else:
        got[4] = shift(got[-2], -2)
    return jnp.concatenate([got[r] if r <= 4 else got[r - NZ] for r in range(NZ)])


def scatter_rows(mine, held=None):
    block = mine.reshape(NZ, mine.shape[0] // NZ, -1)
    rows = block.shape[1] // 2
    total = block[0]
    seconds = []
    for way in (1, -1):
        far = block[4][:rows] if way == 1 else block[4][rows:]
        near = jnp.concatenate([block[way % NZ], block[3 * way % NZ]]).astype(BF)
        near = shift(near, -way).astype(F32)
        far = shift(far.astype(BF), -2 * way).astype(F32)
        total = total + near[: 2 * rows]
        zero = jnp.zeros_like(far)
        relayed = jnp.concatenate([far, zero] if way == 1 else [zero, far])
        seconds.append((block[2 * way % NZ] + near[2 * rows :] + relayed).astype(BF))
    seconds, held = lax.optimization_barrier((seconds, held))
    for way, second in zip((1, -1), seconds):
        total = total + shift(second, -2 * way).astype(F32)
    return (total[:rows] + swap(total[rows:].astype(BF), "xh").astype(F32)).astype(BF), held


def exchange(x):
    return lax.all_to_all(x, COL, 0, 0, tiled=True)


def copies(x):
    return jnp.broadcast_to(x[None], (8,) + x.shape)


def per_device(tokens, gate_up, down_weight, out_grad):
    width = gate_up.shape[2]
    weights = gate_up.reshape(gate_up.shape[0], 2 * width)

    tok = gather_z(together(tokens, swap(tokens, "xh"), weights), True)
    half = tok.shape[0]
    chunk = half // 4

    other, tok = lax.optimization_barrier((out_grad, tok))
    other = swap(other, "xh")
    tok = jnp.concatenate([tok, swap(tok, "core")])
    parts = (jnp.dot(tok, weights, preferred_element_type=F32) * SCALE).astype(F16)
    both = exchange(parts.reshape(8, chunk, -1))

    pair, _ = lax.optimization_barrier((jnp.concatenate([out_grad, other]), parts))
    grad = gather_z(pair, False)
    part = jnp.concatenate(
        product([grad, swap(grad, "core")], down_weight, True, (BF, BF), width)
    ).reshape(8, chunk, width)

    both, part = lax.optimization_barrier((both, part))
    both = both.astype(F32).sum(0) * (1.0 / SCALE)
    gate, up = both[:, :width], both[:, width:]
    squash = jax.nn.sigmoid(gate)
    hidden = (gate * squash * up).astype(BF)
    here = exchange(jnp.concatenate([copies(hidden), part], axis=1))
    hid_grad = here[:, chunk:].astype(F32).sum(0)

    gate_grad = (hid_grad * up * squash * (1.0 + gate * (1.0 - squash))).astype(BF)
    up_grad = (hid_grad * gate * squash).astype(BF)
    send = copies(jnp.concatenate([gate_grad, up_grad], axis=1))
    hidden = [here[i : i + 4, :chunk].reshape(half, width) for i in (0, 4)]
    send, hidden = lax.optimization_barrier((send, hidden))
    grads = exchange(send).reshape(2 * half, 2 * width)

    kept, sent = product(hidden, down_weight, False, (F32, BF), 256)
    block_out, grads = scatter_rows(kept + swap(sent, "core").astype(F32), grads)
    out = lax.dot_general(grads, weights, LAST, preferred_element_type=F32)
    out = out[:half] + swap(out[half:].astype(BF), "core").astype(F32)
    grad_tokens, _ = scatter_rows(out)
    return block_out, grad_tokens


def solution(mesh):
    fine = Mesh(mesh.devices.reshape(8, 2, 2, 2, 4), ("z", "xh", "core", "xl", "y"))
    return jax.shard_map(
        per_device,
        mesh=fine,
        in_specs=(P(ROW, COL), P(COL, None, ROW), P(ROW, COL), P(ROW, COL)),
        out_specs=(P(ROW, COL), P(ROW, COL)),
        check_vma=False,
    )
```

```python
import jax
import jax.numpy as jnp
from jax import lax
from jax.experimental import pallas as pl
from jax.experimental.pallas import tpu as pltpu
from jax.sharding import Mesh, PartitionSpec as P

BF = jnp.bfloat16
F16 = jnp.float16
F32 = jnp.float32
ROW, COL = ("z", "xh", "core"), ("xl", "y")
LAST = (((1,), (1,)), ((), ()))
SWAP = [(0, 1), (1, 0)]
NZ = 8
SCALE = 64.0


def product(xs, w, turned, types, width):
    depth = xs[0].shape[1]
    n = w.shape[0] if turned else w.shape[1]
    dims = (((1,), (1 if turned else 0,)), ((), ()))

    def body(*refs):
        w_ref = refs[len(xs)]
        for x_ref, o_ref in zip(refs, refs[len(xs) + 1 :]):
            o_ref[...] = lax.dot_general(
                x_ref[...], w_ref[...], dims, preferred_element_type=F32
            ).astype(o_ref.dtype)

    if turned:
        w_spec = pl.BlockSpec((width, depth), lambda i: (i, 0))
    else:
        w_spec = pl.BlockSpec((depth, width), lambda i: (0, i))
    rows = sum(x.shape[0] for x in xs)
    return pl.pallas_call(
        body,
        grid=(n // width,),
        in_specs=[pl.BlockSpec(x.shape, lambda i: (0, 0)) for x in xs] + [w_spec],
        out_specs=[pl.BlockSpec((x.shape[0], width), lambda i: (0, i)) for x in xs],
        out_shape=[jax.ShapeDtypeStruct((x.shape[0], n), t) for x, t in zip(xs, types)],
        compiler_params=pltpu.CompilerParams(vmem_limit_bytes=40 << 20),
        cost_estimate=pl.CostEstimate(
            flops=rows, bytes_accessed=rows * depth,
            transcendentals=0,
        ),
    )(*xs, w)


def swap(x, axis):
    return lax.ppermute(x, axis, SWAP)


def shift(x, by):
    return lax.ppermute(x, "z", [(i, (i - by) % NZ) for i in range(NZ)])


def gather_z(pair, even):
    half = pair.shape[0] // 2
    got = {0: pair}
    for r in (2, -2, 1, -1):
        got[r] = shift(pair, r)
    got[3], got[-3] = shift(got[2], 1), shift(got[-2], -1)
    if even:
        got[4] = jnp.concatenate([shift(got[2][:half], 2), shift(got[-2][half:], -2)])
    else:
        got[4] = shift(got[-2], -2)
    return jnp.concatenate([got[r] if r <= 4 else got[r - NZ] for r in range(NZ)])


def first_round(mine):
    block = mine.reshape(NZ, mine.shape[0] // NZ, -1)
    rows = block.shape[1] // 2
    total = block[0]
    seconds = []
    for way in (1, -1):
        far = block[4][:rows] if way == 1 else block[4][rows:]
        near = jnp.concatenate([block[way % NZ], block[3 * way % NZ]]).astype(BF)
        near = shift(near, -way).astype(F32)
        far = shift(far.astype(BF), -2 * way).astype(F32)
        total = total + near[: 2 * rows]
        zero = jnp.zeros_like(far)
        relayed = jnp.concatenate([far, zero] if way == 1 else [zero, far])
        seconds.append((block[2 * way % NZ] + near[2 * rows :] + relayed).astype(BF))
    return total, seconds


def second_round(seconds):
    return [shift(second, -2 * way) for way, second in zip((1, -1), seconds)]


def last_round(total, seconds):
    total = total + seconds[0].astype(F32) + seconds[1].astype(F32)
    rows = total.shape[0] // 2
    return (total[:rows] + swap(total[rows:].astype(BF), "xh").astype(F32)).astype(BF)


def exchange(x):
    return lax.all_to_all(x, COL, 0, 0, tiled=True)


def copies(x):
    return jnp.broadcast_to(x[None], (8,) + x.shape)


def per_device(tokens, gate_up, down_weight, out_grad):
    width = gate_up.shape[2]
    weights = gate_up.reshape(gate_up.shape[0], 2 * width)

    n = tokens.shape[0]
    other = swap(jnp.concatenate([tokens, out_grad]), "xh")
    tok = gather_z(jnp.concatenate([tokens, other[:n]]), True)
    half = tok.shape[0]
    chunk = half // 4

    tok = jnp.concatenate([tok, swap(tok, "core")])
    parts = (jnp.dot(tok, weights, preferred_element_type=F32) * SCALE).astype(F16)
    both = exchange(parts.reshape(8, chunk, -1))

    pair, _ = lax.optimization_barrier((jnp.concatenate([out_grad, other[n:]]), parts))
    grad = gather_z(pair, False)
    part = jnp.concatenate(
        product([grad, swap(grad, "core")], down_weight, True, (BF, BF), width)
    ).reshape(8, chunk, width)

    both, part = lax.optimization_barrier((both, part))
    both = both.astype(F32).sum(0) * (1.0 / SCALE)
    gate, up = both[:, :width], both[:, width:]
    squash = jax.nn.sigmoid(gate)
    hidden = (gate * squash * up).astype(BF)
    here = exchange(jnp.concatenate([copies(hidden), part], axis=1))
    hid_grad = here[:, chunk:].astype(F32).sum(0)

    gate_grad = (hid_grad * up * squash * (1.0 + gate * (1.0 - squash))).astype(BF)
    up_grad = (hid_grad * gate * squash).astype(BF)
    send = copies(jnp.concatenate([gate_grad, up_grad], axis=1))
    hidden = [here[i : i + 4, :chunk].reshape(half, width) for i in (0, 4)]
    send, hidden = lax.optimization_barrier((send, hidden))
    grads = exchange(send).reshape(2 * half, 2 * width)

    kept, sent = product(hidden, down_weight, False, (F32, BF), 512)
    total, seconds = first_round(kept + swap(sent, "core").astype(F32))
    seconds, grads = lax.optimization_barrier((seconds, grads))
    seconds = second_round(seconds)
    out = lax.dot_general(grads, weights, LAST, preferred_element_type=F32)
    come = swap(out[half:].astype(BF), "core")
    seconds, come = lax.optimization_barrier((seconds, come))
    block_out = last_round(total, seconds)
    total, seconds = first_round(out[:half] + come.astype(F32))
    return block_out, last_round(total, second_round(seconds))


def solution(mesh):
    fine = Mesh(mesh.devices.reshape(8, 2, 2, 2, 4), ("z", "xh", "core", "xl", "y"))
    return jax.shard_map(
        per_device,
        mesh=fine,
        in_specs=(P(ROW, COL), P(COL, None, ROW), P(ROW, COL), P(ROW, COL)),
        out_specs=(P(ROW, COL), P(ROW, COL)),
        check_vma=False,
    )
```

```python
import jax
import jax.numpy as jnp
from jax import lax
from jax.experimental import pallas as pl
from jax.experimental.pallas import tpu as pltpu
from jax.sharding import Mesh, PartitionSpec as P

BF = jnp.bfloat16
F16 = jnp.float16
F32 = jnp.float32
ROW, COL = ("z", "xh", "core"), ("xl", "y")
LAST = (((1,), (1,)), ((), ()))
SWAP = [(0, 1), (1, 0)]
NZ = 8
SCALE = 64.0


def product(xs, w, turned, types, width):
    depth = xs[0].shape[1]
    n = w.shape[0] if turned else w.shape[1]
    dims = (((1,), (1 if turned else 0,)), ((), ()))

    def body(*refs):
        w_ref = refs[len(xs)]
        for x_ref, o_ref in zip(refs, refs[len(xs) + 1 :]):
            o_ref[...] = lax.dot_general(
                x_ref[...], w_ref[...], dims, preferred_element_type=F32
            ).astype(o_ref.dtype)

    if turned:
        w_spec = pl.BlockSpec((width, depth), lambda i: (i, 0))
    else:
        w_spec = pl.BlockSpec((depth, width), lambda i: (0, i))
    rows = sum(x.shape[0] for x in xs)
    return pl.pallas_call(
        body,
        grid=(n // width,),
        in_specs=[pl.BlockSpec(x.shape, lambda i: (0, 0)) for x in xs] + [w_spec],
        out_specs=[pl.BlockSpec((x.shape[0], width), lambda i: (0, i)) for x in xs],
        out_shape=[jax.ShapeDtypeStruct((x.shape[0], n), t) for x, t in zip(xs, types)],
        compiler_params=pltpu.CompilerParams(vmem_limit_bytes=40 << 20),
        cost_estimate=pl.CostEstimate(
            flops=rows, bytes_accessed=rows * depth,
            transcendentals=0,
        ),
    )(*xs, w)


def swap(x, axis):
    return lax.ppermute(x, axis, SWAP)


def shift(x, by):
    return lax.ppermute(x, "z", [(i, (i - by) % NZ) for i in range(NZ)])


def gather_z(pair, even):
    half = pair.shape[0] // 2
    got = {0: pair}
    for r in (2, -2, 1, -1):
        got[r] = shift(pair, r)
    got[3], got[-3] = shift(got[2], 1), shift(got[-2], -1)
    if even:
        got[4] = jnp.concatenate([shift(got[2][:half], 2), shift(got[-2][half:], -2)])
    else:
        got[4] = shift(got[-2], -2)
    return jnp.concatenate([got[r] if r <= 4 else got[r - NZ] for r in range(NZ)])


def first_round(mine):
    block = mine.reshape(NZ, mine.shape[0] // NZ, -1)
    rows = block.shape[1] // 2
    total = block[0]
    seconds = []
    for way in (1, -1):
        far = block[4][:rows] if way == 1 else block[4][rows:]
        near = jnp.concatenate([block[way % NZ], block[3 * way % NZ]]).astype(BF)
        near = shift(near, -way).astype(F32)
        far = shift(far.astype(BF), -2 * way).astype(F32)
        total = total + near[: 2 * rows]
        zero = jnp.zeros_like(far)
        relayed = jnp.concatenate([far, zero] if way == 1 else [zero, far])
        seconds.append((block[2 * way % NZ] + near[2 * rows :] + relayed).astype(BF))
    return total, seconds


def second_round(seconds):
    return [shift(second, -2 * way) for way, second in zip((1, -1), seconds)]


def added(total, seconds):
    return total + seconds[0].astype(F32) + seconds[1].astype(F32)


def last_round(sums):
    rows = sums[0].shape[0] // 2
    come = swap(jnp.concatenate([x[rows:] for x in sums]).astype(BF), "xh").astype(F32)
    return [(x[:rows] + come[i * rows : (i + 1) * rows]).astype(BF) for i, x in enumerate(sums)]


def exchange(x):
    return lax.all_to_all(x, COL, 0, 0, tiled=True)


def copies(x):
    return jnp.broadcast_to(x[None], (8,) + x.shape)


def per_device(tokens, gate_up, down_weight, out_grad):
    width = gate_up.shape[2]
    weights = gate_up.reshape(gate_up.shape[0], 2 * width)

    n = tokens.shape[0]
    other = swap(jnp.concatenate([tokens, out_grad]), "xh")
    tok = gather_z(jnp.concatenate([tokens, other[:n]]), True)
    half = tok.shape[0]
    chunk = half // 4

    tok = jnp.concatenate([tok, swap(tok, "core")])
    parts = (jnp.dot(tok, weights, preferred_element_type=F32) * SCALE).astype(F16)
    both = exchange(parts.reshape(8, chunk, -1))

    pair, _ = lax.optimization_barrier((jnp.concatenate([out_grad, other[n:]]), parts))
    grad = gather_z(pair, False)
    part = jnp.concatenate(
        product([grad, swap(grad, "core")], down_weight, True, (BF, BF), width)
    ).reshape(8, chunk, width)

    both, part = lax.optimization_barrier((both, part))
    both = both.astype(F32).sum(0) * (1.0 / SCALE)
    gate, up = both[:, :width], both[:, width:]
    squash = jax.nn.sigmoid(gate)
    hidden = (gate * squash * up).astype(BF)
    here = exchange(jnp.concatenate([copies(hidden), part], axis=1))
    hid_grad = here[:, chunk:].astype(F32).sum(0)

    gate_grad = (hid_grad * up * squash * (1.0 + gate * (1.0 - squash))).astype(BF)
    up_grad = (hid_grad * gate * squash).astype(BF)
    send = copies(jnp.concatenate([gate_grad, up_grad], axis=1))
    hidden = [here[i : i + 4, :chunk].reshape(half, width) for i in (0, 4)]
    send, hidden = lax.optimization_barrier((send, hidden))
    grads = exchange(send).reshape(2 * half, 2 * width)

    kept, sent = product(hidden, down_weight, False, (F32, BF), 512)
    total, seconds = first_round(kept + swap(sent, "core").astype(F32))
    seconds, grads = lax.optimization_barrier((second_round(seconds), grads))
    total = added(total, seconds)
    out = lax.dot_general(grads, weights, LAST, preferred_element_type=F32)
    out = out[:half] + swap(out[half:].astype(BF), "core").astype(F32)
    last, seconds = first_round(out)
    block_out, grad_tokens = last_round([total, added(last, second_round(seconds))])
    return block_out, grad_tokens


def solution(mesh):
    fine = Mesh(mesh.devices.reshape(8, 2, 2, 2, 4), ("z", "xh", "core", "xl", "y"))
    return jax.shard_map(
        per_device,
        mesh=fine,
        in_specs=(P(ROW, COL), P(COL, None, ROW), P(ROW, COL), P(ROW, COL)),
        out_specs=(P(ROW, COL), P(ROW, COL)),
        check_vma=False,
    )
```

```python
import jax
import jax.numpy as jnp
from jax import lax
from jax.experimental import pallas as pl
from jax.experimental.pallas import tpu as pltpu
from jax.sharding import Mesh, PartitionSpec as P

BF = jnp.bfloat16
F16 = jnp.float16
F32 = jnp.float32
ROW, COL = ("z", "xh", "core"), ("xl", "y")
LAST = (((1,), (1,)), ((), ()))
SWAP = [(0, 1), (1, 0)]
NZ = 8
SCALE = 64.0


def product(xs, w, turned, types, width):
    depth = xs[0].shape[1]
    n = w.shape[0] if turned else w.shape[1]
    dims = (((1,), (1 if turned else 0,)), ((), ()))

    def body(*refs):
        w_ref = refs[len(xs)]
        for x_ref, o_ref in zip(refs, refs[len(xs) + 1 :]):
            o_ref[...] = lax.dot_general(
                x_ref[...], w_ref[...], dims, preferred_element_type=F32
            ).astype(o_ref.dtype)

    if turned:
        w_spec = pl.BlockSpec((width, depth), lambda i: (i, 0))
    else:
        w_spec = pl.BlockSpec((depth, width), lambda i: (0, i))
    rows = sum(x.shape[0] for x in xs)
    return pl.pallas_call(
        body,
        grid=(n // width,),
        in_specs=[pl.BlockSpec(x.shape, lambda i: (0, 0)) for x in xs] + [w_spec],
        out_specs=[pl.BlockSpec((x.shape[0], width), lambda i: (0, i)) for x in xs],
        out_shape=[jax.ShapeDtypeStruct((x.shape[0], n), t) for x, t in zip(xs, types)],
        compiler_params=pltpu.CompilerParams(vmem_limit_bytes=40 << 20),
        cost_estimate=pl.CostEstimate(
            flops=rows, bytes_accessed=rows * depth,
            transcendentals=0,
        ),
    )(*xs, w)


def swap(x, axis):
    return lax.ppermute(x, axis, SWAP)


def shift(x, by):
    return lax.ppermute(x, "z", [(i, (i - by) % NZ) for i in range(NZ)])


def gather_z(pair, even):
    half = pair.shape[0] // 2
    got = {0: pair}
    for r in (2, -2, 1, -1):
        got[r] = shift(pair, r)
    got = lax.optimization_barrier(got)
    got[3], got[-3] = shift(got[2], 1), shift(got[-2], -1)
    if even:
        got[4] = jnp.concatenate([shift(got[2][:half], 2), shift(got[-2][half:], -2)])
    else:
        got[4] = shift(got[-2], -2)
    return jnp.concatenate([got[r] if r <= 4 else got[r - NZ] for r in range(NZ)])


def first_round(mine):
    block = mine.reshape(NZ, mine.shape[0] // NZ, -1)
    rows = block.shape[1] // 2
    total = block[0]
    seconds = []
    for way in (1, -1):
        far = block[4][:rows] if way == 1 else block[4][rows:]
        near = jnp.concatenate([block[way % NZ], block[3 * way % NZ]]).astype(BF)
        near = shift(near, -way).astype(F32)
        far = shift(far.astype(BF), -2 * way).astype(F32)
        total = total + near[: 2 * rows]
        zero = jnp.zeros_like(far)
        relayed = jnp.concatenate([far, zero] if way == 1 else [zero, far])
        seconds.append((block[2 * way % NZ] + near[2 * rows :] + relayed).astype(BF))
    return total, seconds


def second_round(seconds):
    return [shift(second, -2 * way) for way, second in zip((1, -1), seconds)]


def added(total, seconds):
    return total + seconds[0].astype(F32) + seconds[1].astype(F32)


def halves(total):
    rows = total.shape[0] // 2
    return total[:rows], swap(total[rows:].astype(BF), "xh")


def joined(kept, come):
    return (kept + come.astype(F32)).astype(BF)


def exchange(x):
    return lax.all_to_all(x, COL, 0, 0, tiled=True)


def copies(x):
    return jnp.broadcast_to(x[None], (8,) + x.shape)


def per_device(tokens, gate_up, down_weight, out_grad):
    width = gate_up.shape[2]
    weights = gate_up.reshape(gate_up.shape[0], 2 * width)

    n = tokens.shape[0]
    other = swap(jnp.concatenate([tokens, out_grad]), "xh")
    tok = gather_z(jnp.concatenate([tokens, other[:n]]), True)
    half = tok.shape[0]
    chunk = half // 4

    tok = jnp.concatenate([tok, swap(tok, "core")])
    parts = (jnp.dot(tok, weights, preferred_element_type=F32) * SCALE).astype(F16)
    both = exchange(parts.reshape(8, chunk, -1))

    pair, _ = lax.optimization_barrier((jnp.concatenate([out_grad, other[n:]]), parts))
    grad = gather_z(pair, False)
    part = jnp.concatenate(
        product([grad, swap(grad, "core")], down_weight, True, (BF, BF), width)
    ).reshape(8, chunk, width)

    both, part = lax.optimization_barrier((both, part))
    both = both.astype(F32).sum(0) * (1.0 / SCALE)
    gate, up = both[:, :width], both[:, width:]
    squash = jax.nn.sigmoid(gate)
    hidden = (gate * squash * up).astype(BF)
    here = exchange(jnp.concatenate([copies(hidden), part], axis=1))
    hid_grad = here[:, chunk:].astype(F32).sum(0)

    gate_grad = (hid_grad * up * squash * (1.0 + gate * (1.0 - squash))).astype(BF)
    up_grad = (hid_grad * gate * squash).astype(BF)
    send = copies(jnp.concatenate([gate_grad, up_grad], axis=1))
    hidden = [here[i : i + 4, :chunk].reshape(half, width) for i in (0, 4)]
    send, hidden = lax.optimization_barrier((send, hidden))
    grads = exchange(send).reshape(2 * half, 2 * width)

    kept, sent = product(hidden, down_weight, False, (F32, BF), 512)
    total, seconds = first_round(kept + swap(sent, "core").astype(F32))
    seconds, grads = lax.optimization_barrier((second_round(seconds), grads))
    kept, come = halves(added(total, seconds))
    out = lax.dot_general(grads, weights, LAST, preferred_element_type=F32)
    sent, come = lax.optimization_barrier((swap(out[half:].astype(BF), "core"), come))
    total, seconds = first_round(out[:half] + sent.astype(F32))
    return joined(kept, come), joined(*halves(added(total, second_round(seconds))))


def solution(mesh):
    fine = Mesh(mesh.devices.reshape(8, 2, 2, 2, 4), ("z", "xh", "core", "xl", "y"))
    return jax.shard_map(
        per_device,
        mesh=fine,
        in_specs=(P(ROW, COL), P(COL, None, ROW), P(ROW, COL), P(ROW, COL)),
        out_specs=(P(ROW, COL), P(ROW, COL)),
        check_vma=False,
    )
```

```python
import jax
import jax.numpy as jnp
from jax import lax
from jax.experimental import pallas as pl
from jax.experimental.pallas import tpu as pltpu
from jax.sharding import Mesh, PartitionSpec as P

BF = jnp.bfloat16
F16 = jnp.float16
F32 = jnp.float32
ROW, COL = ("z", "xh", "core"), ("xl", "y")
LAST = (((1,), (1,)), ((), ()))
SWAP = [(0, 1), (1, 0)]
NZ = 8
SCALE = 64.0


def product(xs, w, turned, types, width):
    depth = xs[0].shape[1]
    n = w.shape[0] if turned else w.shape[1]
    dims = (((1,), (1 if turned else 0,)), ((), ()))

    def body(*refs):
        w_ref = refs[len(xs)]
        for x_ref, o_ref in zip(refs, refs[len(xs) + 1 :]):
            o_ref[...] = lax.dot_general(
                x_ref[...], w_ref[...], dims, preferred_element_type=F32
            ).astype(o_ref.dtype)

    if turned:
        w_spec = pl.BlockSpec((width, depth), lambda i: (i, 0))
    else:
        w_spec = pl.BlockSpec((depth, width), lambda i: (0, i))
    rows = sum(x.shape[0] for x in xs)
    return pl.pallas_call(
        body,
        grid=(n // width,),
        in_specs=[pl.BlockSpec(x.shape, lambda i: (0, 0)) for x in xs] + [w_spec],
        out_specs=[pl.BlockSpec((x.shape[0], width), lambda i: (0, i)) for x in xs],
        out_shape=[jax.ShapeDtypeStruct((x.shape[0], n), t) for x, t in zip(xs, types)],
        compiler_params=pltpu.CompilerParams(vmem_limit_bytes=40 << 20),
        cost_estimate=pl.CostEstimate(
            flops=rows, bytes_accessed=rows * depth,
            transcendentals=0,
        ),
    )(*xs, w)


def swap(x, axis):
    return lax.ppermute(x, axis, SWAP)


def shift(x, by):
    return lax.ppermute(x, "z", [(i, (i - by) % NZ) for i in range(NZ)])


def gather_z(pair, even):
    half = pair.shape[0] // 2
    got = {0: pair}
    for r in (2, -2, 1, -1):
        got[r] = shift(pair, r)
    got[3], got[-3] = shift(got[2], 1), shift(got[-2], -1)
    if even:
        got[4] = jnp.concatenate([shift(got[2][:half], 2), shift(got[-2][half:], -2)])
    else:
        got[4] = shift(got[-2], -2)
    return jnp.concatenate([got[r] if r <= 4 else got[r - NZ] for r in range(NZ)])


def first_round(mine):
    block = mine.reshape(NZ, mine.shape[0] // NZ, -1)
    rows = block.shape[1] // 2
    total = block[0]
    seconds = []
    for way in (1, -1):
        far = block[4][:rows] if way == 1 else block[4][rows:]
        near = jnp.concatenate([block[way % NZ], block[3 * way % NZ]]).astype(BF)
        near = shift(near, -way).astype(F32)
        far = shift(far.astype(BF), -2 * way).astype(F32)
        total = total + near[: 2 * rows]
        zero = jnp.zeros_like(far)
        relayed = jnp.concatenate([far, zero] if way == 1 else [zero, far])
        seconds.append((block[2 * way % NZ] + near[2 * rows :] + relayed).astype(BF))
    return total, seconds


def second_round(seconds):
    return [shift(second, -2 * way) for way, second in zip((1, -1), seconds)]


def added(total, seconds):
    return total + seconds[0].astype(F32) + seconds[1].astype(F32)


def last_round(sums):
    rows = sums[0].shape[0] // 2
    come = swap(jnp.concatenate([x[rows:] for x in sums]).astype(BF), "xh").astype(F32)
    return [(x[:rows] + come[i * rows : (i + 1) * rows]).astype(BF) for i, x in enumerate(sums)]


def exchange(x):
    return lax.all_to_all(x, COL, 0, 0, tiled=True)


def copies(x):
    return jnp.broadcast_to(x[None], (8,) + x.shape)


def per_device(tokens, gate_up, down_weight, out_grad):
    width = gate_up.shape[2]
    weights = gate_up.reshape(gate_up.shape[0], 2 * width)

    n = tokens.shape[0]
    other = swap(jnp.concatenate([tokens, out_grad]), "xh")
    tok = gather_z(jnp.concatenate([tokens, other[:n]]), True)
    half = tok.shape[0]
    chunk = half // 4

    tok = jnp.concatenate([tok, swap(tok, "core")])
    parts = (jnp.dot(tok, weights, preferred_element_type=F32) * SCALE).astype(F16)
    both = exchange(parts.reshape(8, chunk, -1))

    pair, _ = lax.optimization_barrier((jnp.concatenate([out_grad, other[n:]]), parts))
    grad = gather_z(pair, False)
    part = jnp.concatenate(
        product([grad, swap(grad, "core")], down_weight, True, (BF, BF), width)
    ).reshape(8, chunk, width)

    both = both.astype(F32).sum(0) * (1.0 / SCALE)
    gate, up = both[:, :width], both[:, width:]
    squash = jax.nn.sigmoid(gate)
    hidden = (gate * squash * up).astype(BF)
    here = exchange(jnp.concatenate([copies(hidden), part], axis=1))
    hid_grad = here[:, chunk:].astype(F32).sum(0)

    gate_grad = (hid_grad * up * squash * (1.0 + gate * (1.0 - squash))).astype(BF)
    up_grad = (hid_grad * gate * squash).astype(BF)
    send = copies(jnp.concatenate([gate_grad, up_grad], axis=1))
    hidden = [here[i : i + 4, :chunk].reshape(half, width) for i in (0, 4)]
    send, hidden = lax.optimization_barrier((send, hidden))
    grads = exchange(send).reshape(2 * half, 2 * width)

    kept, sent = product(hidden, down_weight, False, (F32, BF), 512)
    total, seconds = first_round(kept + swap(sent, "core").astype(F32))
    seconds, grads = lax.optimization_barrier((second_round(seconds), grads))
    total = added(total, seconds)
    out = lax.dot_general(grads, weights, LAST, preferred_element_type=F32)
    out = out[:half] + swap(out[half:].astype(BF), "core").astype(F32)
    last, seconds = first_round(out)
    block_out, grad_tokens = last_round([total, added(last, second_round(seconds))])
    return block_out, grad_tokens


def solution(mesh):
    fine = Mesh(mesh.devices.reshape(8, 2, 2, 2, 4), ("z", "xh", "core", "xl", "y"))
    return jax.shard_map(
        per_device,
        mesh=fine,
        in_specs=(P(ROW, COL), P(COL, None, ROW), P(ROW, COL), P(ROW, COL)),
        out_specs=(P(ROW, COL), P(ROW, COL)),
        check_vma=False,
    )
```
